1024 devices in a mesh: row: 32 (over y, x_lo, core), col: 32 (over x_hi, z).
Axes of the slice: x: 4 (x_hi: 2, x_lo: 2; x = x_hi * 2 + x_lo), y: 8, z: 16, core: 2. Of those that a mesh axis runs over, the one named last changes fastest.
Arguments:
- iterate: bfloat16 [3584, 18432], P('row', 'col'), may hold values from -0.03125 to 0.03125
Outputs:
- update: float32 [3584, 18432], P('row', 'col')
The draws below stay inside these ranges and needn't reach their ends.
All inputs are finite; a program needn't handle non-finite values.
Results may differ from the reference program's by a relative error of at most 0.0045.
Values may be sent and summed in bfloat16 or wider, within the bound.
No kernel may reach another device: no remote copies, remote signals or barrier semaphores. Data moves between devices by JAX's collectives and lax.ppermute only.
A program may use at most 32 MiB of HBM per device.

```python
import math
import jax
import jax.numpy as jnp

M = 3584
N = 18432


def block_levels(stream_key, extent, split, smallest, top_value):
    def one(dim, shards_of):
        heights = jax.random.uniform(jax.random.fold_in(jax.random.fold_in(stream_key, 6), dim), (shards_of,), jnp.float32, smallest / len(split), top_value / len(split))
        return jnp.repeat(jnp.exp(heights), extent[dim] // shards_of).reshape((-1,) + (1,) * (len(extent) - dim - 1))

    level = one(*split[0])
    for cut in split[1:]:
        level = level * one(*cut)
    return level


def centred(own_key, shape, scale, reach, split=(), dtype=jnp.bfloat16):
    values = scale * jax.random.normal(own_key, shape, jnp.float32)
    if split:
        values = values * block_levels(own_key, shape, split, -0.22, 0.18)
    return jnp.clip(values, -reach, reach).astype(dtype)


def setup_inputs(seed: int = 0) -> dict:
    key_of = jax.random.split(jax.random.key(seed), 2)
    iterate = centred(key_of[0], (M, N), (2 * N) ** -0.5, 0.03125, ((0, 32), (1, 32)))
    return dict(iterate=iterate)


def reference(iterate):
    gram = jnp.dot(iterate, iterate.T, preferred_element_type=jnp.float32).astype(jnp.bfloat16)
    square = jnp.dot(gram, gram, preferred_element_type=jnp.float32)
    polynomial = (-4.775 * gram.astype(jnp.float32) + 2.0315 * square).astype(jnp.bfloat16)
    product = jnp.dot(polynomial, iterate, preferred_element_type=jnp.float32)
    scaling = 0.2 * math.sqrt(max(M, N))
    return scaling * (3.4445 * iterate.astype(jnp.float32) + product)
```

```python
import math

import jax
import jax.numpy as jnp
from jax import lax
from jax.sharding import Mesh
from jax.sharding import PartitionSpec as P

M = 3584
N = 18432
BLOCK = 112
HALF = 56
SWAP = [(0, 1), (1, 0)]


def f32(value):
    return value.astype(jnp.float32)


def bf16(value):
    return value.astype(jnp.bfloat16)


def dot(a, b, dims):
    return lax.dot_general(a, b, ((dims[0:1], dims[1:2]), ((), ())), preferred_element_type=jnp.float32)


def swap(value, axis):
    return lax.ppermute(value, axis, SWAP)


def gather_panel(block):
    own = lax.all_gather(block, "y", axis=0)
    return own, swap(own, "c")


def apply_gram(gram, own, other):
    width = own.shape[-1]
    near, far = gram[: 8 * BLOCK], gram[8 * BLOCK :]
    part = dot(near, own.reshape(8 * BLOCK, width), (0, 0))
    part = part + dot(far, other.reshape(8 * BLOCK, width), (0, 0))
    part = part.reshape(2, BLOCK, width)
    return part[0] + f32(swap(bf16(part[1]), "l"))


def on_device(iterate):
    h = lax.axis_index("h")
    band = jnp.concatenate([iterate, swap(iterate, "l")], axis=0)
    own, other = gather_panel(iterate)
    width = iterate.shape[-1]

    def gram_half(which):
        parts = []
        for panel in (own, other):
            rows = lax.dynamic_slice_in_dim(panel, which * HALF, HALF, 1)
            parts.append(dot(rows.reshape(8 * HALF, width), band, (1, 1)))
        return jnp.concatenate(parts, axis=0)

    received = swap(bf16(gram_half(1 - h)), "h")
    pieces = bf16(gram_half(h) + f32(received)).reshape(16, HALF, 2 * BLOCK)
    pieces = lax.all_to_all(pieces, "z", 0, 0, tiled=True)
    gram = bf16(f32(pieces).sum(0))
    gram = lax.all_gather(gram, "h", axis=0)
    gram = lax.all_gather(gram, "z", axis=0)
    gram = gram.reshape(16 * BLOCK, 2 * BLOCK)

    first = apply_gram(gram, own, other)
    second = apply_gram(gram, *gather_panel(bf16(first)))
    scaling = 0.2 * math.sqrt(max(M, N))
    return scaling * (3.4445 * f32(iterate) - 4.775 * first + 2.0315 * second)


def solution(mesh):
    grid = Mesh(mesh.devices.reshape(8, 2, 2, 2, 16), ("y", "l", "c", "h", "z"))
    spec = P(("y", "l", "c"), ("h", "z"))
    return jax.shard_map(
        on_device, mesh=grid, in_specs=(spec,), out_specs=spec, check_vma=False
    )
```
